256 devices in a mesh: dense: 2 (over core), tp: 8 (over z), attn: 16 (over x, y).
Axes of the slice: x: 4, y: 4, z: 8, core: 2. Of those that a mesh axis runs over, the one named last changes fastest.
Arguments:
- hidden: bfloat16 [128, 8192], P('dense', 'attn'), may hold values from -6 to 6
- w_query: bfloat16 [8192, 8192], P('attn', 'tp'), may hold values from -0.0625 to 0.0625
- w_key: bfloat16 [8192, 1024], P('attn', 'tp'), may hold values from -0.0625 to 0.0625
- w_value: bfloat16 [8192, 1024], P('attn', 'tp'), may hold values from -0.0625 to 0.0625
- b_query: bfloat16 [8192], P('tp'), may hold values from -3 to 3
- b_key: bfloat16 [1024], P('tp'), may hold values from -6 to 6
- b_value: bfloat16 [1024], P('tp'), may hold values from -6 to 6
- w_out: bfloat16 [8192, 8192], P('tp', 'attn'), may hold values from -0.0625 to 0.0625
- k_cache: bfloat16 [128, 4096, 1024], P(('dense', 'attn'), None, 'tp'), may hold values from -60 to 60
- value_cache: bfloat16 [128, 4096, 1024], P(('dense', 'attn'), None, 'tp'), may hold values from -6 to 6
- slot_seq: int32 [128], P(('dense', 'attn')), may hold values from 0 to 31, as said below
- slot_len: int32 [128], P(('dense', 'attn')), may hold values from 1 to 4096, as said below
Outputs:
- attn_out: bfloat16 [128, 8192], P('dense', 'attn')
The draws below stay inside these ranges and needn't reach their ends.
Inputs may be any that keep to these rules, and one draw needn't show every extreme that they name: `slot_seq`: every transcript is named by one or more slots. `slot_len`: some slot holds exactly 4096 live tokens.
All inputs are finite; a program needn't handle non-finite values.
Results may differ from the reference program's by a relative error of at most 0.012.
The reference program's roundings to bfloat16 on the way count: a program that leaves them out, or rounds other values in their place, can miss the bound.
Values may be sent and summed in bfloat16 or wider, within the bound.
A program may use at most 128 MiB of HBM per device.

```python
import jax
import jax.numpy as jnp
from jax import lax

D = 8192
H = 64
KEY_HEADS = 8
HEAD_SIZE = 128
STEPS = 4
SLOT_TOKENS = 4096
TRANSCRIPT_COUNT = 32
SLOT_COUNT = 128


def draw_slot_seq(key, part):
    key = jax.random.fold_in(key, 11)
    first_part, second_part = jax.random.split(key)
    slot_order = jnp.arange(SLOT_COUNT, dtype=jnp.int32)
    spare_slots = jax.random.randint(first_part, (SLOT_COUNT,), 0, TRANSCRIPT_COUNT, dtype=jnp.int32)
    named = jnp.where(slot_order < TRANSCRIPT_COUNT, slot_order, spare_slots).astype(jnp.int32)
    slot_shuffle = jax.random.permutation(second_part, SLOT_COUNT)
    return named[slot_shuffle]


def draw_slot_len(key, part):
    key = jax.random.fold_in(key, 23)
    first_part, second_part = jax.random.split(key)
    slot_order = jnp.arange(SLOT_COUNT, dtype=jnp.int32)
    token_counts = jax.random.randint(first_part, (SLOT_COUNT,), 1, SLOT_TOKENS + 1, dtype=jnp.int32)
    picked_slots = jax.random.randint(second_part, (), 0, SLOT_COUNT, dtype=jnp.int32)
    return jnp.where(slot_order == picked_slots, SLOT_TOKENS, token_counts).astype(jnp.int32)


def draw_k_cache(key, part):
    key = jax.random.fold_in(key, 37)
    first_part = jax.random.fold_in(key, 0)
    array_shape = (SLOT_COUNT, SLOT_TOKENS, KEY_HEADS * HEAD_SIZE)
    values = jnp.clip(jax.random.normal(first_part, array_shape, jnp.float32), -4.0, 4.0)
    return values.astype(jnp.bfloat16)


def strengthened(entries, stream_key, source, target, shards_of, factor):
    owner, partner = [(jnp.arange(entries.shape[position]) // (entries.shape[position] // shards_of)).reshape([-1 if axis == position else 1 for axis in range(entries.ndim)]) for position in (source, target)]
    chosen = jax.random.permutation(stream_key, shards_of)[partner]
    strong = (owner == chosen) | (owner == (partner + shards_of // 2) % shards_of)
    return jnp.where(strong, factor * entries, entries)


def shard_levels(rng, shape, pieces, smallest, largest):
    loudness, own = 1.0, jax.random.fold_in(rng, 6)
    for dim, blocks in pieces:
        steps = jnp.exp(jax.random.uniform(jax.random.fold_in(own, dim), (blocks,), jnp.float32, smallest / len(pieces), largest / len(pieces)))
        loudness = loudness * jnp.repeat(steps, shape[dim] // blocks).reshape([-1 if axis == dim else 1 for axis in range(len(shape))])
    return loudness


def noise(stream_key, extent, scale, bound, shards=(), kind=jnp.bfloat16):
    values = scale * jax.random.normal(stream_key, extent, jnp.float32)
    if shards:
        values = values * shard_levels(stream_key, extent, shards, -0.22, 0.18)
    return jnp.clip(values, -bound, bound).astype(kind)


def bell_draw_with(stream_key, shape, scale, most, shards, heavy, held_as=jnp.bfloat16):
    entries = scale * jax.random.normal(stream_key, shape, jnp.float32)
    if shards:
        entries = entries * shard_levels(stream_key, shape, shards, -0.22, 0.18)
    return jnp.clip(strengthened(entries, jax.random.fold_in(stream_key, 3), *heavy), -most, most).astype(held_as)


def setup_inputs(seed: int = 0) -> dict:
    seeds = jax.random.split(jax.random.key(seed), 13)
    hidden = bell_draw_with(seeds[0], (TRANSCRIPT_COUNT * STEPS, D), 1.0, 6.0, ((0, 2), (1, 16)), (1, 0, 16, 2.0))
    w_query = noise(seeds[1], (D, H * HEAD_SIZE), D ** -0.5, 0.0625, ((0, 16), (1, 8)))
    w_key = noise(seeds[2], (D, KEY_HEADS * HEAD_SIZE), D ** -0.5, 0.0625, ((0, 16), (1, 8)))
    w_value = noise(seeds[3], (D, KEY_HEADS * HEAD_SIZE), D ** -0.5, 0.0625, ((0, 16), (1, 8)))
    b_query = noise(seeds[4], (H * HEAD_SIZE,), 0.5, 3.0, ((0, 8),))
    b_key = noise(seeds[5], (KEY_HEADS * HEAD_SIZE,), 1.0, 6.0, ((0, 8),))
    b_value = noise(seeds[6], (KEY_HEADS * HEAD_SIZE,), 1.0, 6.0, ((0, 8),))
    w_out = noise(seeds[7], (H * HEAD_SIZE, D), (H * HEAD_SIZE) ** -0.5, 0.0625, ((0, 8), (1, 16)))
    k_cache = draw_k_cache(jax.random.fold_in(seeds[12], 71), 0)
    value_cache = noise(seeds[9], (SLOT_COUNT, SLOT_TOKENS, KEY_HEADS * HEAD_SIZE), 1.0, 6.0, ((0, 32), (2, 8)))
    slot_seq = draw_slot_seq(jax.random.fold_in(seeds[12], 71), 0)
    slot_len = draw_slot_len(jax.random.fold_in(seeds[12], 71), 0)
    return dict(hidden=hidden, w_query=w_query, w_key=w_key, w_value=w_value, b_query=b_query, b_key=b_key, b_value=b_value, w_out=w_out, k_cache=k_cache, value_cache=value_cache, slot_seq=slot_seq, slot_len=slot_len)


NEG = -1.0e30


def project(hidden, weight, bias):
    total = jnp.dot(hidden, weight, preferred_element_type=jnp.float32)
    return (total + bias.astype(jnp.float32)).astype(jnp.bfloat16)


def reference(hidden, w_query, w_key, w_value, b_query, b_key, b_value, w_out, k_cache, value_cache, slot_seq, slot_len):
    group = H // KEY_HEADS
    scale = HEAD_SIZE ** -0.5
    query = project(hidden, w_query, b_query).reshape(TRANSCRIPT_COUNT, STEPS, KEY_HEADS, group, HEAD_SIZE)
    new_key = project(hidden, w_key, b_key).reshape(TRANSCRIPT_COUNT, STEPS, KEY_HEADS, HEAD_SIZE)
    new_value = project(hidden, w_value, b_value).reshape(TRANSCRIPT_COUNT, STEPS, KEY_HEADS, HEAD_SIZE)

    def per_slot(items):
        keys, values, owner, live = items
        rows = lax.dynamic_index_in_dim(query, owner, 0, keepdims=False).astype(jnp.float32)
        keys = keys.reshape(SLOT_TOKENS, KEY_HEADS, HEAD_SIZE).astype(jnp.float32)
        values = values.reshape(SLOT_TOKENS, KEY_HEADS, HEAD_SIZE).astype(jnp.float32)
        scores = jnp.einsum("sghd,cgd->ghsc", rows, keys) * scale
        valid = jnp.arange(SLOT_TOKENS, dtype=jnp.int32) < live
        scores = jnp.where(valid, scores, NEG)
        top = jnp.max(scores, axis=-1)
        weights = jnp.exp(scores - top[..., None])
        total = jnp.sum(weights, axis=-1)
        rounded = lax.optimization_barrier(weights.astype(jnp.bfloat16)).astype(jnp.float32)
        mixed = jnp.einsum("ghsc,cgd->ghsd", rounded, values)
        return top, total, mixed

    slot_top, slot_total, slot_mixed = lax.map(per_slot, (k_cache, value_cache, slot_seq, slot_len))

    scores = jnp.einsum("tsghd,tugd->tghsu", query.astype(jnp.float32), new_key.astype(jnp.float32)) * scale
    causal = jnp.arange(STEPS)[:, None] >= jnp.arange(STEPS)[None, :]
    scores = jnp.where(causal, scores, NEG)
    new_top = jnp.max(scores, axis=-1)
    weights = jnp.exp(scores - new_top[..., None])
    new_total = jnp.sum(weights, axis=-1)
    rounded = lax.optimization_barrier(weights.astype(jnp.bfloat16)).astype(jnp.float32)
    new_mixed = jnp.einsum("tghsu,tugd->tghsd", rounded, new_value.astype(jnp.float32))

    onehot = slot_seq[:, None] == jnp.arange(TRANSCRIPT_COUNT, dtype=jnp.int32)[None, :]
    spread = jnp.where(onehot[:, :, None, None, None], slot_top[:, None], NEG)
    best = jnp.maximum(jnp.max(spread, axis=0), new_top)
    factor = jnp.exp(slot_top - best[slot_seq])
    total = jax.ops.segment_sum(factor * slot_total, slot_seq, TRANSCRIPT_COUNT)
    mixed = jax.ops.segment_sum(factor[..., None] * slot_mixed, slot_seq, TRANSCRIPT_COUNT)
    own = jnp.exp(new_top - best)
    total = total + own * new_total
    mixed = mixed + own[..., None] * new_mixed
    attention = mixed / total[..., None]
    attention = jnp.transpose(attention, (0, 3, 1, 2, 4)).reshape(TRANSCRIPT_COUNT * STEPS, H * HEAD_SIZE).astype(jnp.bfloat16)
    return jnp.dot(attention, w_out, preferred_element_type=jnp.float32).astype(jnp.bfloat16)
```

```python
import jax
import jax.numpy as jnp
from jax import lax
from jax.experimental import pallas as pl
from jax.experimental.pallas import tpu as pltpu
from jax.sharding import PartitionSpec as P

MESH = pl.DeviceIdType.MESH
F32 = jnp.float32
BF16 = jnp.bfloat16

STEPS = 4
GROUP = 8
E = 128
ROWS = STEPS * GROUP
PART = STEPS * (GROUP + 2)
TOKENS = 4096
CHUNK = 1024
SLOTS = 4
NA = 16
NZ = 8
NEG = -1e30
SCALE = E**-0.5 * 1.4426950408889634
FAR = sorted(
    range(1, NA), key=lambda k: -(min(k // 4, 4 - k // 4) + min(k % 4, 4 - k % 4))
)
FAR_Z = sorted(range(1, NZ), key=lambda k: -min(k, 8 - k))


def kernel(
    h_hbm, wq_hbm, wk_hbm, wv_hbm, bq_hbm, bk_hbm, bv_hbm, wo_hbm, kc_hbm, vc_hbm, seq, live,
    out,
    h, wq, wk, wv, bq, bk, bv, wo, kb, vb,
    parts, parts_in, total, q_all, scores, slot_o, slot_ml, seq_in, messages, mixed_out, mixed_in,
    att, att_wide, terms, terms_in, done,
    load_sem, s1, r1, s2, r2, s2f, r2f, ss, rs, sq, rq, s3, r3, s4, r4, s5, r5, s6, r6,
):
    d, z, a = lax.axis_index("dense"), lax.axis_index("tp"), lax.axis_index("attn")
    x, y = a // 4, a % 4
    sibling = (1 - d, z, a)

    def at(k):
        return ((x + k // 4) % 4) * 4 + (y + k % 4) % 4

    def before(k):
        return ((x + 4 - k // 4) % 4) * 4 + (y + 4 - k % 4) % 4

    barrier = pltpu.get_barrier_semaphore()
    for k in FAR:
        pl.semaphore_signal(barrier, inc=1, device_id=(d, z, at(k)), device_id_type=MESH)
    for k in FAR_Z:
        pl.semaphore_signal(barrier, inc=1, device_id=(d, (z + k) % NZ, a), device_id_type=MESH)
    pl.semaphore_signal(barrier, inc=1, device_id=sibling, device_id_type=MESH)

    first = [
        pltpu.make_async_copy(src, dst, load_sem.at[i])
        for i, (src, dst) in enumerate(
            [(h_hbm, h), (wq_hbm, wq), (wk_hbm, wk), (wv_hbm, wv), (bq_hbm, bq), (bk_hbm, bk), (bv_hbm, bv)]
        )
    ]
    later = [
        pltpu.make_async_copy(src, dst, load_sem.at[7 + i])
        for i, (src, dst) in enumerate([(kc_hbm, kb), (vc_hbm, vb), (wo_hbm, wo)])
    ]
    for copy in first:
        copy.start()
    for copy in first:
        copy.wait()
    for copy in later:
        copy.start()

    rows = h[...]
    for c in range(0, GROUP, 2):
        pair = jnp.dot(rows, wq[:, c * E : (c + 2) * E], preferred_element_type=F32)
        parts[pl.ds(c, 64, stride=10), :] = pair[:, :E]
        parts[pl.ds(c + 1, 64, stride=10), :] = pair[:, E:]
    parts[pl.ds(8, 64, stride=10), :] = jnp.dot(rows, wk[...], preferred_element_type=F32)
    parts[pl.ds(9, 64, stride=10), :] = jnp.dot(rows, wv[...], preferred_element_type=F32)

    def block(t):
        return pl.ds(pl.multiple_of(t * PART, PART), PART)

    pl.semaphore_wait(barrier, NA - 1 + NZ - 1 + 1)
    copies1 = [
        pltpu.make_async_remote_copy(
            parts.at[block(at(k))], parts_in.at[k], s1.at[k], r1.at[k], device_id=(d, z, at(k)), device_id_type=MESH
        )
        for k in FAR
    ]
    for copy in copies1:
        copy.start()
    seq_copy = pltpu.make_async_remote_copy(
        seq, seq_in, sq, rq, device_id=sibling, device_id_type=MESH
    )
    seq_copy.start()

    for c in range(GROUP):
        total[pl.ds(c, STEPS, stride=10), :] = jnp.broadcast_to(bq[pl.ds(c * E, E)].astype(F32)[None, :], (STEPS, E))
    total[pl.ds(8, STEPS, stride=10), :] = jnp.broadcast_to(bk[...].astype(F32)[None, :], (STEPS, E))
    total[pl.ds(9, STEPS, stride=10), :] = jnp.broadcast_to(bv[...].astype(F32)[None, :], (STEPS, E))
    so_far = parts[block(a), :]
    for copy, k in reversed(list(zip(copies1, FAR))):
        copy.wait_recv()
        so_far = so_far + parts_in[k]
    total[...] = total[...] + so_far
    own = d * NA + a
    for s in range(STEPS):
        scores[s * GROUP : (s + 1) * GROUP, :E] = total[s * 10 : s * 10 + GROUP, :]
    query = scores[:ROWS, :E].astype(BF16)
    q_all[own] = query

    copies2 = [
        pltpu.make_async_remote_copy(
            q_all.at[own], q_all.at[own], s2.at[k], r2.at[k], device_id=(d, z, at(k)), device_id_type=MESH
        )
        for k in FAR
    ]
    for copy in copies2:
        copy.start()

    def forward(k):
        t = d * NA + before(k)
        return pltpu.make_async_remote_copy(
            q_all.at[t], q_all.at[t], s2f.at[k], r2f.at[k], device_id=sibling, device_id_type=MESH
        )

    forwards = [forward(k) for k in range(NA)]
    forwards[0].start()

    wide = query.astype(F32)
    new_key = total[pl.ds(8, STEPS, stride=10), :].astype(BF16).astype(F32)
    new_value = total[pl.ds(9, STEPS, stride=10), :].astype(BF16).astype(F32)
    step_of = lax.broadcasted_iota(jnp.int32, (ROWS, 1), 0) // GROUP
    fresh = [
        jnp.where(step_of >= u, jnp.sum(wide * new_key[u : u + 1, :], axis=1, keepdims=True) * SCALE, NEG)
        for u in range(STEPS)
    ]
    new_top = jnp.maximum(jnp.maximum(fresh[0], fresh[1]), jnp.maximum(fresh[2], fresh[3]))
    new_total = jnp.zeros((ROWS, 1), F32)
    new_mixed = jnp.zeros((ROWS, E), F32)
    for u in range(STEPS):
        weight = jnp.exp2(fresh[u] - new_top)
        new_total = new_total + weight
        new_mixed = new_mixed + weight.astype(BF16).astype(F32) * new_value[u : u + 1, :]

    for copy in copies1:
        copy.wait_send()
    seq_copy.wait()
    for copy, k in reversed(list(zip(copies2, FAR))):
        copy.wait_recv()
        forwards[k].start()
    for copy in later:
        copy.wait()
    for k in range(NA):
        forwards[k].wait_recv()

    row64 = lax.broadcasted_iota(jnp.int32, (2 * ROWS, 1), 0)
    lane = lax.broadcasted_iota(jnp.int32, (2 * ROWS, CHUNK), 1)
    slot_copies = []
    for p in range(SLOTS // 2):
        i, j = 2 * p, 2 * p + 1
        qi, qj = q_all[seq[i]], q_all[seq[j]]
        none = jnp.zeros_like(qi)
        left = jnp.concatenate(
            [jnp.concatenate([qi, none], axis=1), jnp.concatenate([none, qj], axis=1)], axis=0
        )
        count = jnp.where(row64 < ROWS, live[i], live[j])
        top = jnp.full((2 * ROWS, E), NEG, F32)
        for c in range(0, TOKENS, CHUNK):
            keys = jnp.concatenate([kb[i, c : c + CHUNK, :], kb[j, c : c + CHUNK, :]], axis=1)
            sc = lax.dot_general(left, keys, (((1,), (1,)), ((), ())), preferred_element_type=F32)
            sc = jnp.where(lane < count - c, sc * SCALE, NEG)
            scores[:, c : c + CHUNK] = sc
            for e in range(0, CHUNK, E):
                top = jnp.maximum(top, sc[:, e : e + E])
        m = jnp.max(top, axis=1, keepdims=True)
        weight_sum = jnp.zeros((2 * ROWS, E), F32)
        mixed = jnp.zeros((2 * ROWS, 2 * E), F32)
        for c in range(0, TOKENS, CHUNK):
            weight = jnp.exp2(scores[:, c : c + CHUNK] - m)
            for e in range(0, CHUNK, E):
                weight_sum = weight_sum + weight[:, e : e + E]
            values = jnp.concatenate([vb[i, c : c + CHUNK, :], vb[j, c : c + CHUNK, :]], axis=1)
            mixed = mixed + jnp.dot(weight.astype(BF16), values, preferred_element_type=F32)
        l = jnp.sum(weight_sum, axis=1, keepdims=True)
        ml = jnp.where(lax.broadcasted_iota(jnp.int32, (2 * ROWS, E), 1) < E // 2, m, l)
        slot_o[p, 0], slot_o[p, 1] = mixed[:ROWS, :E], mixed[ROWS:, E:]
        slot_o[p, 2], slot_o[p, 3] = ml[:ROWS], ml[ROWS:]
        copy = pltpu.make_async_remote_copy(
            slot_o.at[p], slot_ml.at[p], ss.at[p], rs.at[p], device_id=sibling, device_id_type=MESH
        )
        copy.start()
        slot_copies.append(copy)

    for copy in copies2:
        copy.wait_send()
    for copy in forwards:
        copy.wait_send()
    for copy in slot_copies:
        copy.wait()

    owners = [seq[j] for j in range(SLOTS)] + [seq_in[j] for j in range(SLOTS)]
    where = [(slot_o, j) for j in range(SLOTS)] + [(slot_ml, j) for j in range(SLOTS)]
    tops, sums = [], []
    for ref, j in where:
        ml = ref[j // 2, 2 + j % 2]
        tops.append(jnp.broadcast_to(ml[:, :1], (ROWS, E)))
        sums.append(jnp.broadcast_to(ml[:, E // 2 : E // 2 + 1], (ROWS, E)))
    lane16 = lax.broadcasted_iota(jnp.int32, (16, E), 1)

    def tail(level):
        high = level.astype(BF16).astype(F32)
        middle = (level - high).astype(BF16).astype(F32)
        low = level - high - middle
        packed = jnp.zeros((16, E), F32)
        for n, piece in enumerate([high[:16], middle[:16], low[:16], high[16:], middle[16:], low[16:]]):
            packed = jnp.where(lane16 == n, piece, packed)
        return packed.astype(BF16)

    best = []
    for j in range(2 * SLOTS):
        m = tops[j]
        for i in range(2 * SLOTS):
            if i != j:
                m = jnp.maximum(m, jnp.where(owners[i] == owners[j], tops[i], NEG))
        best.append(m)
    factor = [jnp.exp2(tops[j] - best[j]) for j in range(2 * SLOTS)]
    scaled = [factor[j] * where[j][0][where[j][1] // 2, where[j][1] % 2] for j in range(2 * SLOTS)]
    sums = [factor[j] * sums[j] for j in range(2 * SLOTS)]
    for j in range(2 * SLOTS):
        o, l = scaled[j], sums[j]
        for i in range(2 * SLOTS):
            if i != j:
                same = owners[i] == owners[j]
                o = o + jnp.where(same, scaled[i], 0.0)
                l = l + jnp.where(same, sums[i], 0.0)
        messages[j, :ROWS, :] = (o / l).astype(BF16)
        messages[j, ROWS:, :] = tail(best[j] + jnp.log2(l))
    messages[2 * SLOTS, :ROWS, :] = jnp.zeros((ROWS, E), BF16)
    messages[2 * SLOTS, ROWS:, :] = tail(jnp.full((ROWS, E), NEG, F32))

    copies3 = []
    for k in FAR + [0]:
        t = d * NA + at(k)
        index = 2 * SLOTS
        for j in range(2 * SLOTS):
            index = jnp.where(owners[j] == t, j, index)
        if k == 0:
            mixed_in[0] = messages[index]
        else:
            mixed_out[k] = messages[index]
            copy = pltpu.make_async_remote_copy(
                mixed_out.at[k], mixed_in.at[k], s3.at[k], r3.at[k], device_id=(d, z, at(k)), device_id_type=MESH
            )
            copy.start()
            copies3.append(copy)
    for copy in reversed(copies3):
        copy.wait_recv()

    levels = []
    for k in range(NA):
        packed = mixed_in[k, ROWS:, :].astype(F32)
        upper = (packed[:, 0:1] + packed[:, 1:2]) + packed[:, 2:3]
        lower = (packed[:, 3:4] + packed[:, 4:5]) + packed[:, 5:6]
        levels.append(jnp.concatenate([upper, lower], axis=0))
    m = new_top
    for level in levels:
        m = jnp.maximum(m, level)
    weight = jnp.exp2(new_top - m)
    l = weight * new_total
    o = weight * new_mixed
    for k in range(NA):
        weight = jnp.exp2(levels[k] - m)
        l = l + weight
        o = o + weight * mixed_in[k, :ROWS, :].astype(F32)
    att[a] = (o / l).astype(BF16)

    copies4 = [
        pltpu.make_async_remote_copy(
            att.at[a], att.at[a], s4.at[k], r4.at[k], device_id=(d, z, at(k)), device_id_type=MESH
        )
        for k in FAR
    ]
    for copy in copies4:
        copy.start()
    for copy in copies3:
        copy.wait_send()
    for copy in reversed(copies4):
        copy.wait_recv()

    for t in range(NA):
        att_wide[t * ROWS : (t + 1) * ROWS, :] = att[t].astype(F32)
    result = jnp.zeros((64, 512), F32)
    for c in range(0, GROUP, 2):
        heads = jnp.concatenate(
            [
                att_wide[pl.ds(c, 64, stride=GROUP), :].astype(BF16),
                att_wide[pl.ds(c + 1, 64, stride=GROUP), :].astype(BF16),
            ],
            axis=1,
        )
        result = result + jnp.dot(heads, wo[c * E : (c + 2) * E, :], preferred_element_type=F32)
    for b in range(NZ):
        r, c = b % 4, b // 4
        terms[b] = result[r * 16 : (r + 1) * 16, c * 256 : (c + 1) * 256]
    copies5 = [
        pltpu.make_async_remote_copy(
            terms.at[(z + k) % NZ], terms_in.at[k], s5.at[k], r5.at[k],
            device_id=(d, (z + k) % NZ, a), device_id_type=MESH,
        )
        for k in FAR_Z
    ]
    for copy in copies5:
        copy.start()
    for copy in copies4:
        copy.wait_send()
    summed = terms[z]
    for copy, k in reversed(list(zip(copies5, FAR_Z))):
        copy.wait_recv()
        summed = summed + terms_in[k]
    done[...] = summed.astype(BF16)
    copies6 = [
        pltpu.make_async_remote_copy(
            done, out.at[z], s6.at[k], r6.at[k], device_id=(d, (z + k) % NZ, a), device_id_type=MESH
        )
        for k in FAR_Z
    ]
    for copy in copies6:
        copy.start()
    own_copy = pltpu.make_async_copy(done, out.at[z], load_sem.at[10])
    own_copy.start()
    for copy in copies5:
        copy.wait_send()
    own_copy.wait()
    for copy in copies6:
        copy.wait()


def on_device(*args):
    anywhere = pl.BlockSpec(memory_space=pl.ANY)
    scalars = pl.BlockSpec(memory_space=pltpu.SMEM)
    sems = pltpu.SemaphoreType.DMA
    blocks = pl.pallas_call(
        kernel,
        out_shape=jax.ShapeDtypeStruct((NZ, 16, 256), BF16),
        in_specs=[anywhere] * 10 + [scalars] * 2,
        out_specs=anywhere,
        scratch_shapes=[
            *(pltpu.VMEM(arg.shape, arg.dtype) for arg in args[:10]),
            pltpu.VMEM((NA * PART, E), F32),
            pltpu.VMEM((NA, PART, E), F32),
            pltpu.VMEM((PART, E), F32),
            pltpu.VMEM((2 * NA, ROWS, E), BF16),
            pltpu.VMEM((2 * ROWS, TOKENS), F32),
            pltpu.VMEM((2, 4, ROWS, E), F32),
            pltpu.VMEM((2, 4, ROWS, E), F32),
            pltpu.SMEM((SLOTS,), jnp.int32),
            pltpu.VMEM((2 * SLOTS + 1, ROWS + 16, E), BF16),
            pltpu.VMEM((NA, ROWS + 16, E), BF16),
            pltpu.VMEM((NA, ROWS + 16, E), BF16),
            pltpu.VMEM((NA, ROWS, E), BF16),
            pltpu.VMEM((NA * ROWS, E), F32),
            pltpu.VMEM((NZ, 16, 256), F32),
            pltpu.VMEM((NZ, 16, 256), F32),
            pltpu.VMEM((16, 256), BF16),
            sems((11,)),
            *[sems((NA,))] * 6,
            *[sems((2,))] * 2,
            sems(()),
            sems(()),
            *[sems((NA,))] * 4,
            *[sems((NZ,))] * 4,
        ],
        compiler_params=pltpu.CompilerParams(
            collective_id=0, has_side_effects=True, vmem_limit_bytes=56 << 20
        ),
        name="decode",
    )(*args)
    return blocks.reshape(2, 4, 16, 256).transpose(1, 2, 0, 3).reshape(64, 512)


def solution(mesh):
    in_specs = (
        P("dense", "attn"),
        P("attn", "tp"),
        P("attn", "tp"),
        P("attn", "tp"),
        P("tp"),
        P("tp"),
        P("tp"),
        P("tp", "attn"),
        P(("dense", "attn"), None, "tp"),
        P(("dense", "attn"), None, "tp"),
        P(("dense", "attn")),
        P(("dense", "attn")),
    )
    return jax.shard_map(
        on_device, mesh=mesh, in_specs=in_specs, out_specs=P("dense", "attn"), check_vma=False
    )
```

```python
import jax
import jax.numpy as jnp
from jax import lax
from jax.experimental import pallas as pl
from jax.experimental.pallas import tpu as pltpu
from jax.sharding import PartitionSpec as P

MESH = pl.DeviceIdType.MESH
F32 = jnp.float32
BF16 = jnp.bfloat16

STEPS = 4
GROUP = 8
E = 128
ROWS = STEPS * GROUP
STRIDE = GROUP + 2
PART = STEPS * STRIDE
TOKENS = 4096
CHUNK = 1024
SLOTS = 4
NA = 16
NZ = 8
NEG = -1e30
SCALE = E**-0.5 * 1.4426950408889634
FAR = [10, 6, 14, 9, 11, 5, 15, 7, 13, 2, 8, 1, 12, 3, 4]
FAR_Z = sorted(range(1, NZ), key=lambda k: -min(k, 8 - k))


def kernel(
    h_hbm, wq_hbm, wk_hbm, wv_hbm, bq_hbm, bk_hbm, bv_hbm, wo_hbm, kc_hbm, vc_hbm, seq_hbm, live_hbm,
    out,
    h, wq, wk, wv, bq, bk, bv, wo, kb, vb, seq, live,
    parts, parts_in, total, q_all, scores, slot_o, slot_in, seq_in, messages, mixed_out, mixed_in,
    att, att_wide, terms, terms_out, terms_in, done,
    load_sem, s1, r1, s2, r2, s2f, r2f, ss, rs, sq, rq, s3, r3, s4, r4, s5, r5, s6, r6,
):
    d, z, a = lax.axis_index("dense"), lax.axis_index("tp"), lax.axis_index("attn")
    x, y = a // 4, a % 4
    sibling = (1 - d, z, a)

    def at(k):
        return ((x + k // 4) % 4) * 4 + (y + k % 4) % 4

    def before(k):
        return ((x + 4 - k // 4) % 4) * 4 + (y + 4 - k % 4) % 4

    first = [
        pltpu.make_async_copy(src, dst, load_sem.at[i])
        for i, (src, dst) in enumerate(
            [(h_hbm, h), (wq_hbm, wq), (wk_hbm, wk), (wv_hbm, wv), (bq_hbm, bq), (bk_hbm, bk), (bv_hbm, bv)]
        )
    ]
    later = [
        pltpu.make_async_copy(src, dst, load_sem.at[7 + i])
        for i, (src, dst) in enumerate(
            [(seq_hbm, seq), (live_hbm, live), (kc_hbm, kb), (vc_hbm, vb), (wo_hbm, wo)]
        )
    ]
    for copy in first + later:
        copy.start()
    barrier = pltpu.get_barrier_semaphore()
    for k in FAR:
        pl.semaphore_signal(barrier, inc=1, device_id=(d, z, at(k)), device_id_type=MESH)
    for k in FAR:
        pl.semaphore_signal(barrier, inc=1, device_id=(1 - d, z, at(k)), device_id_type=MESH)
    for k in FAR_Z:
        pl.semaphore_signal(barrier, inc=1, device_id=(d, (z + k) % NZ, a), device_id_type=MESH)
    pl.semaphore_signal(barrier, inc=1, device_id=sibling, device_id_type=MESH)

    for copy in first:
        copy.wait()

    rows = h[...]
    for c in range(0, GROUP, 2):
        pair = jnp.dot(rows, wq[:, c * E : (c + 2) * E], preferred_element_type=F32)
        parts[pl.ds(c, 64, stride=STRIDE), :] = pair[:, :E]
        parts[pl.ds(c + 1, 64, stride=STRIDE), :] = pair[:, E:]
    parts[pl.ds(8, 64, stride=STRIDE), :] = jnp.dot(rows, wk[...], preferred_element_type=F32)
    parts[pl.ds(9, 64, stride=STRIDE), :] = jnp.dot(rows, wv[...], preferred_element_type=F32)

    def block(t):
        return pl.ds(pl.multiple_of(t * PART, PART), PART)

    pl.semaphore_wait(barrier, 2 * (NA - 1) + NZ - 1 + 1)
    copies1 = [
        pltpu.make_async_remote_copy(
            parts.at[block(at(k))], parts_in.at[k], s1.at[k], r1.at[k], device_id=(d, z, at(k)), device_id_type=MESH
        )
        for k in FAR
    ]
    for copy in copies1:
        copy.start()
    later[0].wait()
    seq_copy = pltpu.make_async_remote_copy(
        seq, seq_in, sq, rq, device_id=sibling, device_id_type=MESH
    )
    seq_copy.start()

    for c in range(GROUP):
        total[pl.ds(c, STEPS, stride=STRIDE), :] = jnp.broadcast_to(bq[pl.ds(c * E, E)].astype(F32)[None, :], (STEPS, E))
    total[pl.ds(8, STEPS, stride=STRIDE), :] = jnp.broadcast_to(bk[...].astype(F32)[None, :], (STEPS, E))
    total[pl.ds(9, STEPS, stride=STRIDE), :] = jnp.broadcast_to(bv[...].astype(F32)[None, :], (STEPS, E))
    so_far = parts[block(a), :]
    for copy, k in reversed(list(zip(copies1, FAR))):
        copy.wait_recv()
        so_far = so_far + parts_in[k]
    total[...] = total[...] + so_far
    own = d * NA + a
    for s in range(STEPS):
        scores[0, s * GROUP : (s + 1) * GROUP, :E] = total[s * STRIDE : s * STRIDE + GROUP, :]
    query = scores[0, :ROWS, :E].astype(BF16)
    q_all[own] = query

    copies2 = [
        pltpu.make_async_remote_copy(
            q_all.at[own], q_all.at[own], s2.at[k], r2.at[k], device_id=(d, z, at(k)), device_id_type=MESH
        )
        for k in FAR
    ]
    across = [
        pltpu.make_async_remote_copy(
            q_all.at[own], q_all.at[own], s2f.at[k], r2f.at[k], device_id=(1 - d, z, at(k)), device_id_type=MESH
        )
        for k in FAR
    ]
    for copy, other in zip(copies2, across):
        copy.start()
        other.start()
    across.append(
        pltpu.make_async_remote_copy(
            q_all.at[own], q_all.at[own], s2f.at[0], r2f.at[0], device_id=sibling, device_id_type=MESH
        )
    )
    across[-1].start()

    wide = query.astype(F32)
    new_key = total[pl.ds(8, STEPS, stride=STRIDE), :].astype(BF16).astype(F32)
    new_value = total[pl.ds(9, STEPS, stride=STRIDE), :].astype(BF16).astype(F32)
    step_of = lax.broadcasted_iota(jnp.int32, (ROWS, 1), 0) // GROUP
    fresh = [
        jnp.where(step_of >= u, jnp.sum(wide * new_key[u : u + 1, :], axis=1, keepdims=True) * SCALE, NEG)
        for u in range(STEPS)
    ]
    new_top = jnp.maximum(jnp.maximum(fresh[0], fresh[1]), jnp.maximum(fresh[2], fresh[3]))
    new_total = jnp.zeros((ROWS, 1), F32)
    new_mixed = jnp.zeros((ROWS, E), F32)
    for u in range(STEPS):
        weight = jnp.exp2(fresh[u] - new_top)
        new_total = new_total + weight
        new_mixed = new_mixed + weight.astype(BF16).astype(F32) * new_value[u : u + 1, :]

    for copy in copies1:
        copy.wait_send()
    seq_copy.wait()
    for copy in copies2:
        copy.wait_recv()
    for copy in later[1:]:
        copy.wait()
    for copy in across:
        copy.wait_recv()

    row64 = lax.broadcasted_iota(jnp.int32, (2 * ROWS, 1), 0)
    lane = lax.broadcasted_iota(jnp.int32, (2 * ROWS, CHUNK), 1)
    lane32 = lax.broadcasted_iota(jnp.int32, (ROWS, E), 1)
    ml = jnp.zeros((ROWS, E), F32)
    highest = []
    for p in range(SLOTS // 2):
        i, j = 2 * p, 2 * p + 1
        qi, qj = q_all[seq[i]], q_all[seq[j]]
        none = jnp.zeros_like(qi)
        left = jnp.concatenate(
            [jnp.concatenate([qi, none], axis=1), jnp.concatenate([none, qj], axis=1)], axis=0
        )
        count = jnp.where(row64 < ROWS, live[i], live[j])
        top = jnp.full((2 * ROWS, E), NEG, F32)
        for c in range(0, TOKENS, CHUNK):
            keys = jnp.concatenate([kb[i, c : c + CHUNK, :], kb[j, c : c + CHUNK, :]], axis=1)
            sc = lax.dot_general(left, keys, (((1,), (1,)), ((), ())), preferred_element_type=F32)
            sc = jnp.where(lane < count - c, sc * SCALE, NEG)
            scores[p, :, c : c + CHUNK] = sc
            for e in range(0, CHUNK, E):
                top = jnp.maximum(top, sc[:, e : e + E])
        highest.append(jnp.max(top, axis=1, keepdims=True))
    for p in range(SLOTS // 2):
        i, j, m = 2 * p, 2 * p + 1, highest[p]
        weight_sum = jnp.zeros((2 * ROWS, E), F32)
        mixed = jnp.zeros((2 * ROWS, 2 * E), F32)
        for c in range(0, TOKENS, CHUNK):
            weight = jnp.exp2(scores[p, :, c : c + CHUNK] - m)
            for e in range(0, CHUNK, E):
                weight_sum = weight_sum + weight[:, e : e + E]
            values = jnp.concatenate([vb[i, c : c + CHUNK, :], vb[j, c : c + CHUNK, :]], axis=1)
            mixed = mixed + jnp.dot(weight.astype(BF16), values, preferred_element_type=F32)
        l = jnp.sum(weight_sum, axis=1, keepdims=True)
        slot_o[i], slot_o[j] = mixed[:ROWS, :E], mixed[ROWS:, E:]
        for n, half in ((i, slice(ROWS)), (j, slice(ROWS, None))):
            ml = jnp.where(lane32 == n, m[half], ml)
            ml = jnp.where(lane32 == SLOTS + n, l[half], ml)
    slot_o[SLOTS] = ml
    slot_copy = pltpu.make_async_remote_copy(
        slot_o, slot_in, ss, rs, device_id=sibling, device_id_type=MESH
    )
    slot_copy.start()

    for copy in copies2:
        copy.wait_send()
    for copy in across:
        copy.wait_send()
    slot_copy.wait()

    owners = [seq[j] for j in range(SLOTS)] + [seq_in[j] for j in range(SLOTS)]
    where = [(slot_o, j) for j in range(SLOTS)] + [(slot_in, j) for j in range(SLOTS)]
    tops, sums = [], []
    for ref, j in where:
        ml = ref[SLOTS]
        tops.append(jnp.broadcast_to(ml[:, j : j + 1], (ROWS, E)))
        sums.append(jnp.broadcast_to(ml[:, SLOTS + j : SLOTS + j + 1], (ROWS, E)))
    lane16 = lax.broadcasted_iota(jnp.int32, (16, E), 1)

    def tail(level):
        high = level.astype(BF16).astype(F32)
        middle = (level - high).astype(BF16).astype(F32)
        low = level - high - middle
        packed = jnp.zeros((16, E), F32)
        for n, piece in enumerate([high[:16], middle[:16], low[:16], high[16:], middle[16:], low[16:]]):
            packed = jnp.where(lane16 == n, piece, packed)
        return packed.astype(BF16)

    best = []
    for j in range(2 * SLOTS):
        m = tops[j]
        for i in range(2 * SLOTS):
            if i != j:
                m = jnp.maximum(m, jnp.where(owners[i] == owners[j], tops[i], NEG))
        best.append(m)
    factor = [jnp.exp2(tops[j] - best[j]) for j in range(2 * SLOTS)]
    scaled = [factor[j] * where[j][0][where[j][1]] for j in range(2 * SLOTS)]
    sums = [factor[j] * sums[j] for j in range(2 * SLOTS)]
    for j in range(2 * SLOTS):
        o, l = scaled[j], sums[j]
        for i in range(2 * SLOTS):
            if i != j:
                same = owners[i] == owners[j]
                o = o + jnp.where(same, scaled[i], 0.0)
                l = l + jnp.where(same, sums[i], 0.0)
        messages[j, :ROWS, :] = (o / l).astype(BF16)
        messages[j, ROWS:, :] = tail(best[j] + jnp.log2(l))
    messages[2 * SLOTS, :ROWS, :] = jnp.zeros((ROWS, E), BF16)
    messages[2 * SLOTS, ROWS:, :] = tail(jnp.full((ROWS, E), NEG, F32))

    copies3 = []
    for k in FAR + [0]:
        t = d * NA + at(k)
        index = 2 * SLOTS
        for j in range(2 * SLOTS):
            index = jnp.where(owners[j] == t, j, index)
        if k == 0:
            mixed_in[0] = messages[index]
        else:
            mixed_out[k] = messages[index]
            copy = pltpu.make_async_remote_copy(
                mixed_out.at[k], mixed_in.at[k], s3.at[k], r3.at[k], device_id=(d, z, at(k)), device_id_type=MESH
            )
            copy.start()
            copies3.append(copy)
    for copy in reversed(copies3):
        copy.wait_recv()
    levels = []
    for k in range(NA):
        packed = mixed_in[k, ROWS:, :].astype(F32)
        upper = jnp.sum(jnp.where(lane16 < 3, packed, 0.0), axis=1, keepdims=True)
        lower = jnp.sum(jnp.where(lane16 < 3, 0.0, packed), axis=1, keepdims=True)
        levels.append(jnp.concatenate([upper, lower], axis=0))
    m = new_top
    for level in levels:
        m = jnp.maximum(m, level)
    weight = jnp.exp2(new_top - m)
    l = weight * new_total
    o = weight * new_mixed
    for k, level in enumerate(levels):
        weight = jnp.exp2(level - m)
        l = l + weight
        o = o + weight * mixed_in[k, :ROWS, :].astype(F32)
    att[a] = (o / l).astype(BF16)

    copies4 = [
        pltpu.make_async_remote_copy(
            att.at[a], att.at[a], s4.at[k], r4.at[k], device_id=(d, z, at(k)), device_id_type=MESH
        )
        for k in FAR
    ]
    for copy in copies4:
        copy.start()
    for copy in copies3:
        copy.wait_send()
    for n, k in enumerate([0] + FAR[::-1]):
        if k:
            copies4[NA - 1 - n].wait_recv()
        t = before(k)
        att_wide[pl.ds(pl.multiple_of(t * ROWS, ROWS), ROWS), :] = att[t].astype(F32)
    result = jnp.zeros((64, 512), F32)
    for c in range(0, GROUP, 2):
        heads = jnp.concatenate(
            [
                att_wide[pl.ds(c, 64, stride=GROUP), :].astype(BF16),
                att_wide[pl.ds(c + 1, 64, stride=GROUP), :].astype(BF16),
            ],
            axis=1,
        )
        result = result + jnp.dot(heads, wo[c * E : (c + 2) * E, :], preferred_element_type=F32)
    for b in range(NZ):
        r, c = b % 4, b // 4
        terms[b] = result[r * 16 : (r + 1) * 16, c * 256 : (c + 1) * 256]
        terms_out[b] = terms[b].astype(BF16)
    copies5 = [
        pltpu.make_async_remote_copy(
            terms_out.at[(z + k) % NZ], terms_in.at[k], s5.at[k], r5.at[k],
            device_id=(d, (z + k) % NZ, a), device_id_type=MESH,
        )
        for k in FAR_Z
    ]
    for copy in copies5:
        copy.start()
    for copy in copies4:
        copy.wait_send()
    summed = terms[z]
    for copy, k in reversed(list(zip(copies5, FAR_Z))):
        copy.wait_recv()
        summed = summed + terms_in[k].astype(F32)
    done[...] = summed.astype(BF16)
    place = out.at[pl.ds(pl.multiple_of(z % 4 * 16, 16), 16), pl.ds(pl.multiple_of(z // 4 * 256, 256), 256)]
    copies6 = [
        pltpu.make_async_remote_copy(
            done, place, s6.at[k], r6.at[k], device_id=(d, (z + k) % NZ, a), device_id_type=MESH
        )
        for k in FAR_Z
    ]
    for copy in copies6:
        copy.start()
    own_copy = pltpu.make_async_copy(done, place, load_sem.at[12])
    own_copy.start()
    for copy in copies5:
        copy.wait_send()
    own_copy.wait()
    for copy in copies6:
        copy.wait()


def on_device(*args):
    anywhere = pl.BlockSpec(memory_space=pl.ANY)
    sems = pltpu.SemaphoreType.DMA
    return pl.pallas_call(
        kernel,
        out_shape=pltpu.VMEM((64, 512), BF16),
        in_specs=[anywhere] * 12,
        out_specs=pl.BlockSpec(memory_space=pltpu.VMEM),
        scratch_shapes=[
            *(pltpu.VMEM(arg.shape, arg.dtype) for arg in args[:10]),
            *(pltpu.SMEM(arg.shape, arg.dtype) for arg in args[10:]),
            pltpu.VMEM((NA * PART, E), F32),
            pltpu.VMEM((NA, PART, E), F32),
            pltpu.VMEM((PART, E), F32),
            pltpu.VMEM((2 * NA, ROWS, E), BF16),
            pltpu.VMEM((2, 2 * ROWS, TOKENS), F32),
            pltpu.VMEM((SLOTS + 1, ROWS, E), F32),
            pltpu.VMEM((SLOTS + 1, ROWS, E), F32),
            pltpu.SMEM((SLOTS,), jnp.int32),
            pltpu.VMEM((2 * SLOTS + 1, ROWS + 16, E), BF16),
            pltpu.VMEM((NA, ROWS + 16, E), BF16),
            pltpu.VMEM((NA, ROWS + 16, E), BF16),
            pltpu.VMEM((NA, ROWS, E), BF16),
            pltpu.VMEM((NA * ROWS, E), F32),
            pltpu.VMEM((NZ, 16, 256), F32),
            pltpu.VMEM((NZ, 16, 256), BF16),
            pltpu.VMEM((NZ, 16, 256), BF16),
            pltpu.VMEM((16, 256), BF16),
            sems((13,)),
            *[sems((NA,))] * 6,
            *[sems(())] * 4,
            *[sems((NA,))] * 4,
            *[sems((NZ,))] * 4,
        ],
        compiler_params=pltpu.CompilerParams(
            collective_id=0, has_side_effects=True, vmem_limit_bytes=56 << 20
        ),
        name="decode",
    )(*args)


def solution(mesh):
    in_specs = (
        P("dense", "attn"),
        P("attn", "tp"),
        P("attn", "tp"),
        P("attn", "tp"),
        P("tp"),
        P("tp"),
        P("tp"),
        P("tp", "attn"),
        P(("dense", "attn"), None, "tp"),
        P(("dense", "attn"), None, "tp"),
        P(("dense", "attn")),
        P(("dense", "attn")),
    )
    return jax.shard_map(
        on_device, mesh=mesh, in_specs=in_specs, out_specs=P("dense", "attn"), check_vma=False
    )
```
